128 devices in a mesh: rows: 16 (over z, y), samp: 8 (over x, core).
Axes of the slice: x: 4, y: 4, z: 4, core: 2. Of those that a mesh axis runs over, the one named last changes fastest.
Arguments:
- temp_slab: bfloat16 [128, 65536], P('samp', 'rows'), may hold values from -6 to 6
- stream_slab: bfloat16 [128, 65536], P('samp', 'rows'), may hold values from -6 to 6
- probe: bfloat16 [512, 65536], P(None, 'rows'), may hold values from -6 to 6
Outputs:
- basis: bfloat16 [512, 65536], P(None, 'rows')
- back_image: float32 [512, 65536], P('samp', 'rows')
The draws below stay inside these ranges and needn't reach their ends.
All inputs are finite; a program needn't handle non-finite values.
Results may differ from the reference program's by a relative error of at most 0.0049.
Values may be sent and summed in bfloat16 or wider, within the bound.
No kernel may reach another device: no remote copies, remote signals or barrier semaphores. Data moves between devices by JAX's collectives and lax.ppermute only.
A program may use at most 64 MiB of HBM per device.

```python
import jax
import jax.numpy as jnp
from jax import lax

M = 128
K = 512
RT = 65536


def steps_of(stream_key, dims, pieces, least, largest):
    loudness, own = 1.0, jax.random.fold_in(stream_key, 6)
    for dim, blocks in pieces:
        heights = jnp.exp(jax.random.uniform(jax.random.fold_in(own, dim), (blocks,), jnp.float32, least / len(pieces), largest / len(pieces)))
        loudness = loudness * jnp.repeat(heights, dims[dim] // blocks).reshape([-1 if axis == dim else 1 for axis in range(len(dims))])
    return loudness


def gaussian(stream_key, extent, spread, limit, cuts=(), dtype=jnp.bfloat16):
    array = jax.random.normal(stream_key, extent, jnp.float32) * spread
    if len(cuts) > 0:
        array = steps_of(stream_key, extent, cuts, -0.22, 0.18) * array
    return jnp.clip(array, min=-limit, max=limit).astype(dtype)


def setup_inputs(seed: int = 0) -> dict:
    key_of = jax.random.split(jax.random.key(seed), 4)
    temp_slab = gaussian(key_of[0], (M, RT), 1.0, 6.0, ((0, 8), (1, 16)))
    stream_slab = gaussian(key_of[1], (M, RT), 1.0, 6.0, ((0, 8), (1, 16)))
    probe = gaussian(key_of[2], (K, RT), 1.0, 6.0, ((1, 16),))
    return {"temp_slab": temp_slab, "stream_slab": stream_slab, "probe": probe}


def reference(temp_slab, stream_slab, probe):
    projected = jnp.dot(stream_slab, probe.T, preferred_element_type=jnp.float32).astype(jnp.bfloat16)
    image = jnp.dot(projected.T, temp_slab, preferred_element_type=jnp.float32) / (M - 1.0)
    power = lax.optimization_barrier(jnp.sum(image * image, axis=1))
    basis = (image * jax.lax.rsqrt(power / RT + 1e-06)[:, None]).astype(jnp.bfloat16)
    weights = jnp.dot(temp_slab, basis.T, preferred_element_type=jnp.float32).astype(jnp.bfloat16)
    back_image = jnp.dot(weights.T, stream_slab, preferred_element_type=jnp.float32) / ((M - 1.0) * jnp.sqrt(jnp.float32(RT)))
    return (basis, back_image)
```

```python
import functools

import jax
import jax.numpy as jnp
from jax import lax
from jax.experimental import pallas as pl
from jax.experimental.pallas import tpu as pltpu
from jax.sharding import PartitionSpec as P

F32 = jnp.float32
BF16 = jnp.bfloat16
CORES = 2
HALF_WORK = 1 << 33


def dot(left, right, dims):
    return lax.dot_general(left, right, (dims, ((), ())), preferred_element_type=F32)


def split3(value):
    high = value.astype(BF16)
    rest = value - high.astype(F32)
    mid = rest.astype(BF16)
    return high, mid, (rest - mid.astype(F32)).astype(BF16)


def params(mebibytes):
    return pltpu.CompilerParams(vmem_limit_bytes=mebibytes << 20)


def whole(count):
    return [pl.BlockSpec(memory_space=pltpu.VMEM)] * count


def cost(flops, traffic):
    return pl.CostEstimate(flops=flops, bytes_accessed=traffic, transcendentals=0)


def permute(value, source):
    return lax.ppermute(value, "samp", [(source(n), n) for n in range(lax.axis_size("samp"))])


def chip_step(value, step):
    groups = lax.axis_size("samp")
    return permute(value, lambda n: (n + step * CORES) % groups)


def sibling(value):
    return permute(value, lambda n: n ^ 1)


def around(value, stride, axis="rows"):
    size, span = lax.axis_size(axis), 4 * stride
    steps = [
        [(n // span * span + (n + step * stride) % span, n) for n in range(size)] for step in (1, 3, 2)
    ]
    first, last, opposite = [lax.ppermute(value, axis, pairs) for pairs in steps]
    return [value, first, opposite, last]


def rows_at(place, height):
    return pl.ds(pl.multiple_of(place * height, height), height)


def gram_kernel(part_ref, own_ref, next_ref, half_ref, sibling_ref, message_ref, temp):
    height, columns = part_ref.shape
    chips = temp.shape[0] // height
    span = half_ref.shape[1]
    chip = lax.axis_index("samp") // CORES
    opposite = rows_at(lax.rem(chip + 2, chips), height)
    temp[rows_at(chip, height), :] = own_ref[...]
    temp[rows_at(lax.rem(chip + 1, chips), height), :] = next_ref[...]
    temp[opposite, :] = jnp.zeros(own_ref.shape, BF16)
    temp[opposite, rows_at(chip // 2, span)] = half_ref[...]
    temp[rows_at(lax.rem(chip + 3, chips), height), :] = jnp.zeros(own_ref.shape, BF16)
    mine = jnp.concatenate([own_ref[...], sibling_ref[...]], axis=0)
    gram = dot(mine, temp[...], ((1,), (1,)))
    place = lax.broadcasted_iota(jnp.int32, gram.shape, 1) // height
    gram = jnp.where(place == chip, 0.5 * gram, gram)
    gram = jnp.concatenate([gram[:height], gram[height:]], axis=1)
    message_ref[:, :columns] = part_ref[...]
    message_ref[:, columns:] = gram


def half_kernel(temp_ref, out_ref):
    span = out_ref.shape[1]
    out_ref[...] = temp_ref[:, rows_at(1 - lax.axis_index("samp") // CORES // 2, span)]


def part_kernel(stream_ref, probe_ref, part_ref):
    part_ref[...] = dot(stream_ref[...], probe_ref[...], ((1,), (1,)))


def chip_kernel(temp_ref, temp_sibling_ref, stream_ref, stream_sibling_ref, _, out_ref):
    height = temp_ref.shape[0]
    core = lax.rem(lax.axis_index("samp"), CORES)
    for base, (own, other) in enumerate(((temp_ref, temp_sibling_ref), (stream_ref, stream_sibling_ref))):
        out_ref[rows_at(CORES * base + core, height), :] = own[...]
        out_ref[rows_at(CORES * base + 1 - core, height), :] = other[...]


def copy_kernel(value_ref, _, out_ref):
    out_ref[...] = value_ref[...]


def relay_kernel(both_ref, _, out_ref):
    core = lax.rem(lax.axis_index("samp"), CORES)
    out_ref[...] = both_ref[rows_at(core, out_ref.shape[0]), :]


def order_kernel(chip_ref, beside_ref, beside_sibling_ref, across_ref, across_sibling_ref, out_ref):
    own = lax.axis_index("samp")
    chip, core = own // CORES, lax.rem(own, CORES)
    height = chip_ref.shape[0] // (2 * CORES)
    chips = out_ref.shape[0] // chip_ref.shape[0]

    def put(ref, step, bases):
        place = lax.rem(chip + step, chips)
        for n in range(ref.shape[0] // height):
            base = bases * CORES + n
            out_ref[rows_at(base * chips + place, height), :] = ref[n * height : (n + 1) * height]

    put(chip_ref, 0, 0)
    put(beside_ref, chips - 1 - core * (chips - 2), 0)
    put(beside_sibling_ref, 1 + core * (chips - 2), 0)
    put(across_ref, 2, core)
    put(across_sibling_ref, 2, 1 - core)


def add_kernel(a_ref, b_ref, c_ref, d_ref, out_ref):
    out_ref[...] = (a_ref[...] + b_ref[...]) + (c_ref[...] + d_ref[...])


def sum_kernel(columns, a_ref, b_ref, c_ref, d_ref, message_ref):
    total = (a_ref[...] + b_ref[...]) + (c_ref[...] + d_ref[...])
    pieces = [total[:, :columns].astype(BF16), *split3(total[:, columns:])]
    pieces = jnp.concatenate(pieces, axis=1)
    message_ref[...] = pieces


def collect_kernel(*refs):
    *blocks, out_ref = refs
    height = blocks[0].shape[0]
    chip = lax.axis_index("samp") // CORES
    for step, block in enumerate(blocks):
        out_ref[rows_at(lax.rem(chip + step, len(blocks)), height), :] = block[...]


def output_kernel(columns, scales, *refs):
    near_ref, far_ref, slabs_ref, basis_ref, back_ref, left, gain, weights, message, basis, back, done = refs
    half = near_ref.shape[0]
    samples = CORES * half
    image_scale, back_scale, total_rows = scales
    own = lax.axis_index("samp")
    core = lax.rem(own, CORES)
    message[rows_at(core, half), :] = near_ref[...]
    message[rows_at(1 - core, half), :] = far_ref[...]
    turned = message[:, :columns].astype(F32).T
    left[...] = turned.astype(BF16)
    products = sum(
        message[:, columns + n * samples : columns + (n + 1) * samples].astype(F32) for n in range(3)
    )
    first = lax.broadcasted_iota(jnp.int32, (half, samples), 1) < half
    top = jnp.where(first, products[:half], products[half:])
    bottom = jnp.where(first, products[half:], products[:half])
    bottom = jnp.concatenate([bottom[:, half:], bottom[:, :half]], axis=1)
    gram = jnp.concatenate([top, bottom], axis=0)
    product = sum(dot(left[...], piece, ((1,), (0,))) for piece in split3(gram + gram.T))
    power = jnp.maximum(jnp.sum(product * turned, axis=1, keepdims=True), 0.0)
    power = power * (image_scale * image_scale)
    gain[...] = jnp.broadcast_to(
        image_scale * lax.rsqrt(power / total_rows + 1e-06), gain.shape
    )
    weights[...] = product * gain[...]

    chunks = done.shape[0] - 1
    height = columns // chunks
    copies = []
    for n in range(chunks):
        here = pl.ds(n * height, height)
        image = dot(left[here, :], slabs_ref[:samples, :], ((1,), (0,)))
        scale = jnp.concatenate([gain[here, :]] * (image.shape[1] // samples), axis=1)
        basis[here, :] = (image * scale).astype(BF16)
        copies.append(pltpu.make_async_copy(basis.at[here], basis_ref.at[here], done.at[n]))
        copies[-1].start()
    chosen = weights[rows_at(own, back.shape[0]), :].astype(BF16)
    back[...] = dot(chosen, slabs_ref[samples:, :], ((1,), (0,))) * back_scale
    copies.append(pltpu.make_async_copy(back, back_ref, done.at[chunks]))
    copies[-1].start()
    for copy in copies:
        copy.wait()


def shards(temp_slab, stream_slab, probe):
    height, local_rows = temp_slab.shape
    columns = probe.shape[0]
    groups = lax.axis_size("samp")
    row_groups = lax.axis_size("rows")
    total_rows = local_rows * row_groups
    samples = height * groups
    half = samples // CORES
    wide = columns + samples
    shape = jax.ShapeDtypeStruct

    def call(kernel, name, operands, outs, scratch=(), work=0):
        outs = [shape(*out) for out in outs]
        traffic = sum(value.size * value.dtype.itemsize for value in [*operands, *outs])
        return pl.pallas_call(
            kernel,
            out_shape=tuple(outs),
            in_specs=whole(len(operands)),
            out_specs=tuple(whole(len(outs))),
            scratch_shapes=[pltpu.VMEM(*one) for one in scratch],
            compiler_params=params(16),
            cost_estimate=cost(work, traffic),
            name=name,
        )(*operands)

    packed = columns + 3 * samples
    span = local_rows // 2
    chips = groups // CORES

    (temp_half,) = call(half_kernel, "half", [temp_slab], [((height, span), BF16)], work=HALF_WORK)
    temp_half = chip_step(temp_half, 2)
    temp_next = chip_step(temp_slab, 1)
    temp_sibling = sibling(temp_slab)
    stream_sibling = sibling(stream_slab)
    (part,) = call(
        part_kernel, "part", [stream_slab, probe], [((height, columns), F32)], work=2 * height * columns * local_rows
    )
    (message,) = call(
        gram_kernel,
        "gram",
        [part, temp_slab, temp_next, temp_half, temp_sibling],
        [((height, wide), F32)],
        [((half, local_rows), BF16)],
        4 * height * half * local_rows,
    )
    (chip,) = call(
        chip_kernel,
        "chip",
        [temp_slab, temp_sibling, stream_slab, stream_sibling, message],
        [((4 * height, local_rows), BF16)],
    )
    beside = permute(chip, lambda n: (n - CORES if n % CORES == 0 else n + CORES) % groups)
    (message,) = call(add_kernel, "add", around(message, 1), [((height, wide), F32)])
    (across,) = call(relay_kernel, "relay", [beside, message], [((2 * height, local_rows), BF16)])
    across = permute(across, lambda n: (n - CORES if n % CORES == 0 else n + CORES) % groups)
    beside_sibling = sibling(beside)
    (message,) = call(
        functools.partial(sum_kernel, columns), "total", around(message, 4), [((height, packed), BF16)]
    )
    (later,) = call(copy_kernel, "later", [across, message], [((2 * height, local_rows), BF16)])
    across_sibling = sibling(later)
    (slabs,) = call(
        order_kernel,
        "order",
        [chip, beside, beside_sibling, across, across_sibling],
        [((2 * samples, local_rows), BF16)],
    )
    (message,) = call(collect_kernel, "collect", around(message, CORES, "samp"), [((half, packed), BF16)])
    message_other = sibling(message)

    scales = (
        1.0 / (samples - 1.0),
        1.0 / ((samples - 1.0) * float(total_rows) ** 0.5),
        float(total_rows),
    )
    mine = columns // groups
    chunks = 4
    outs = (shape((columns, local_rows), BF16), shape((mine, local_rows), F32))
    basis, back_image = pl.pallas_call(
        functools.partial(output_kernel, columns, scales),
        out_shape=outs,
        in_specs=whole(3),
        out_specs=tuple([pl.BlockSpec(memory_space=pl.ANY)] * 2),
        scratch_shapes=[
            pltpu.VMEM((columns, samples), BF16),
            pltpu.VMEM((columns, samples), F32),
            pltpu.VMEM((columns, samples), F32),
            pltpu.VMEM((samples, packed), BF16),
            *[pltpu.VMEM(out.shape, out.dtype) for out in outs],
            pltpu.SemaphoreType.DMA((chunks + 1,)),
        ],
        compiler_params=params(40),
        cost_estimate=cost(2 * (columns + mine) * samples * local_rows, 7 << 20),
        name="outputs",
    )(message, message_other, slabs)
    return (basis, back_image)


def solution(mesh):
    return jax.shard_map(
        shards,
        mesh=mesh,
        in_specs=(P("samp", "rows"), P("samp", "rows"), P(None, "rows")),
        out_specs=(P(None, "rows"), P("samp", "rows")),
        check_vma=False,
    )
```

```python
import functools

import jax
import jax.numpy as jnp
from jax import lax
from jax.experimental import pallas as pl
from jax.experimental.pallas import tpu as pltpu
from jax.sharding import PartitionSpec as P

F32 = jnp.float32
BF16 = jnp.bfloat16
CORES = 2
LEAD_WORK = 1 << 33


def dot(left, right, dims):
    return lax.dot_general(left, right, (dims, ((), ())), preferred_element_type=F32)


def split3(value):
    high = value.astype(BF16)
    rest = value - high.astype(F32)
    mid = rest.astype(BF16)
    return high, mid, (rest - mid.astype(F32)).astype(BF16)


def params(mebibytes):
    return pltpu.CompilerParams(vmem_limit_bytes=mebibytes << 20)


def whole(count):
    return [pl.BlockSpec(memory_space=pltpu.VMEM)] * count


def cost(flops, traffic):
    return pl.CostEstimate(flops=flops, bytes_accessed=traffic, transcendentals=0)


def permute(value, source):
    return lax.ppermute(value, "samp", [(source(n), n) for n in range(lax.axis_size("samp"))])


def chip_step(value, step):
    groups = lax.axis_size("samp")
    return permute(value, lambda n: (n + step * CORES) % groups)


def sibling(value):
    return permute(value, lambda n: n ^ 1)


def around(value, stride, axis="rows"):
    size, span = lax.axis_size(axis), 4 * stride
    steps = [
        [(n // span * span + (n + step * stride) % span, n) for n in range(size)] for step in (1, 3, 2)
    ]
    first, last, opposite = [lax.ppermute(value, axis, pairs) for pairs in steps]
    return [value, first, last, opposite]


def rows_at(place, height):
    return pl.ds(pl.multiple_of(place * height, height), height)


def gram_kernel(
    part_ref, own_ref, sibling_ref, before_ref, before_sibling_ref, after_ref, message_ref
):
    height, columns = part_ref.shape
    chips = lax.axis_size("samp") // CORES
    chip = lax.axis_index("samp") // CORES
    mine = jnp.concatenate([own_ref[...], sibling_ref[...]], axis=0)
    others = jnp.concatenate([own_ref[...], after_ref[...]], axis=0)
    near = dot(mine, others, ((1,), (1,)))
    place = lax.broadcasted_iota(jnp.int32, near.shape, 1) // height
    near = jnp.where(place == 0, 0.5 * near, near)
    span = own_ref.shape[1] // 2
    here = rows_at(chip // 2, span)
    across = jnp.concatenate([before_ref[:, here], before_sibling_ref[:, here]], axis=0)
    across = dot(across, after_ref[:, here], ((1,), (1,)))
    gram = jnp.concatenate([near, across, jnp.zeros(across.shape, F32)], axis=1)
    gram = pltpu.roll(jnp.concatenate([gram, gram], axis=1), chip * height, 1)[:, : chips * height]
    message_ref[:, :columns] = part_ref[...]
    message_ref[:, columns:] = jnp.concatenate([gram[:height], gram[height:]], axis=1)


def collect_kernel(*refs):
    *blocks, out_ref = refs
    height = blocks[0].shape[0]
    chip = lax.axis_index("samp") // CORES
    for step, block in zip((0, 1, 3, 2), blocks):
        out_ref[rows_at(lax.rem(chip + step, len(blocks)), height), :] = block[...]


def lead_kernel(out_ref):
    out_ref[...] = jnp.zeros(out_ref.shape, F32)


def copy_kernel(value_ref, _, out_ref):
    out_ref[...] = value_ref[...]


def part_kernel(stream_ref, probe_ref, part_ref):
    part_ref[...] = dot(stream_ref[...], probe_ref[...], ((1,), (1,)))


def beside_kernel(own_ref, sibling_ref, before_ref, after_ref, _, out_ref):
    height = own_ref.shape[0]
    core = lax.rem(lax.axis_index("samp"), CORES)
    out_ref[rows_at(core, height), :] = own_ref[...]
    out_ref[rows_at(1 - core, height), :] = sibling_ref[...]

    @pl.when(core == 0)
    def _():
        out_ref[CORES * height :] = before_ref[...]

    @pl.when(core == 1)
    def _():
        out_ref[CORES * height :] = after_ref[...]


def relay_kernel(beside_ref, _, out_ref):
    core = lax.rem(lax.axis_index("samp"), CORES)
    out_ref[...] = beside_ref[rows_at(core, out_ref.shape[0]), :]


def both_kernel(beside_ref, after_ref, _, out_ref):
    height = after_ref.shape[0]
    out_ref[:-height] = beside_ref[...]
    out_ref[-height:] = after_ref[...]


def order_kernel(
    temp_ref, temp_sibling_ref, before_ref, before_sibling_ref, after_ref, stream_ref, stream_sibling_ref,
    beside_ref, both_ref, across_ref, across_sibling_ref, out_ref,
):
    own = lax.axis_index("samp")
    chip, core = own // CORES, lax.rem(own, CORES)
    height = temp_ref.shape[0]
    chips = out_ref.shape[0] // (2 * CORES * height)

    def put(base, owner, step, value):
        place = (base * CORES + owner) * chips + lax.rem(chip + step, chips)
        out_ref[rows_at(place, height), :] = value

    rows = [slice(n * height, (n + 1) * height) for n in range(2 * CORES)]
    put(0, core, 0, temp_ref[...])
    put(0, 1 - core, 0, temp_sibling_ref[...])
    put(0, core, chips - 1, before_ref[...])
    put(0, 1 - core, chips - 1, before_sibling_ref[...])
    put(0, core, 1, after_ref[...])
    put(0, 1 - core, 1, both_ref[rows[3]])
    put(0, core, 2, beside_ref[rows[2]])
    put(0, 1 - core, 2, both_ref[rows[2]])
    put(1, core, 0, stream_ref[...])
    put(1, 1 - core, 0, stream_sibling_ref[...])
    for n in range(CORES):
        put(1, n, chips - 1 - core * (chips - 2), beside_ref[rows[n]])
        put(1, n, 1 + core * (chips - 2), both_ref[rows[n]])
    put(1, core, 2, across_ref[...])
    put(1, 1 - core, 2, across_sibling_ref[...])


def add_kernel(a_ref, b_ref, c_ref, d_ref, out_ref):
    out_ref[...] = (a_ref[...] + b_ref[...]) + (c_ref[...] + d_ref[...])


def sum_kernel(columns, a_ref, b_ref, c_ref, d_ref, message_ref):
    total = (a_ref[...] + b_ref[...]) + (c_ref[...] + d_ref[...])
    pieces = [total[:, :columns].astype(BF16), *split3(total[:, columns:])]
    pieces = jnp.concatenate(pieces, axis=1)
    message_ref[...] = pieces


def output_kernel(columns, scales, *refs):
    near_ref, far_ref, slabs_ref, basis_ref, back_ref, left, gain, weights, message, basis, back, done = refs
    half = near_ref.shape[0]
    samples = CORES * half
    image_scale, back_scale, total_rows = scales
    own = lax.axis_index("samp")
    core = lax.rem(own, CORES)
    message[rows_at(core, half), :] = near_ref[...]
    message[rows_at(1 - core, half), :] = far_ref[...]
    turned = message[:, :columns].astype(F32).T
    left[...] = turned.astype(BF16)
    products = sum(
        message[:, columns + n * samples : columns + (n + 1) * samples].astype(F32) for n in range(3)
    )
    first = lax.broadcasted_iota(jnp.int32, (half, samples), 1) < half
    top = jnp.where(first, products[:half], products[half:])
    bottom = jnp.where(first, products[half:], products[:half])
    bottom = jnp.concatenate([bottom[:, half:], bottom[:, :half]], axis=1)
    gram = jnp.concatenate([top, bottom], axis=0)
    height = samples // lax.axis_size("samp")
    row, lane = [lax.broadcasted_iota(jnp.int32, gram.shape, axis) // height for axis in (0, 1)]
    chips = half // height
    moves = lax.rem(lane + 2 * chips - row - 2, chips) == 0
    moved = jnp.where(moves, gram, 0.0)
    moved = jnp.concatenate(
        [moved[start : start + size] for base in (0, half) for start, size in ((base + height, half - height), (base, height))],
        axis=0,
    )
    ahead = jnp.concatenate([moved[:, height:], moved[:, :height]], axis=1)
    back_end = jnp.concatenate([moved[:, samples - half + height :], moved[:, : samples - half + height]], axis=1)
    moved = jnp.where(lax.rem(lane, chips) < chips - 1, ahead, back_end)
    gram = jnp.where(moves, 0.0, gram) + moved
    product = sum(dot(left[...], piece, ((1,), (0,))) for piece in split3(gram + gram.T))
    power = jnp.maximum(jnp.sum(product * turned, axis=1, keepdims=True), 0.0)
    power = power * (image_scale * image_scale)
    gain[...] = jnp.broadcast_to(
        image_scale * lax.rsqrt(power / total_rows + 1e-06), gain.shape
    )
    weights[...] = product * gain[...]

    chunks = done.shape[0] - 1
    height = columns // chunks
    copies = []
    for n in range(chunks):
        here = pl.ds(n * height, height)
        image = dot(left[here, :], slabs_ref[:samples, :], ((1,), (0,)))
        scale = jnp.concatenate([gain[here, :]] * (image.shape[1] // samples), axis=1)
        basis[here, :] = (image * scale).astype(BF16)
        copies.append(pltpu.make_async_copy(basis.at[here], basis_ref.at[here], done.at[n]))
        copies[-1].start()
    chosen = weights[rows_at(own, back.shape[0]), :].astype(BF16)
    back[...] = dot(chosen, slabs_ref[samples:, :], ((1,), (0,))) * back_scale
    copies.append(pltpu.make_async_copy(back, back_ref, done.at[chunks]))
    copies[-1].start()
    for copy in copies:
        copy.wait()


def shards(temp_slab, stream_slab, probe):
    height, local_rows = temp_slab.shape
    columns = probe.shape[0]
    groups = lax.axis_size("samp")
    row_groups = lax.axis_size("rows")
    total_rows = local_rows * row_groups
    samples = height * groups
    half = samples // CORES
    wide = columns + samples
    shape = jax.ShapeDtypeStruct

    def call(kernel, name, operands, outs, scratch=(), work=0):
        outs = [shape(*out) for out in outs]
        traffic = sum(value.size * value.dtype.itemsize for value in [*operands, *outs])
        return pl.pallas_call(
            kernel,
            out_shape=tuple(outs),
            in_specs=whole(len(operands)),
            out_specs=tuple(whole(len(outs))),
            scratch_shapes=[pltpu.VMEM(*one) for one in scratch],
            compiler_params=params(16),
            cost_estimate=cost(work, traffic),
            name=name,
        )(*operands)

    slab = ((height, local_rows), BF16)
    packed = columns + 3 * samples

    (lead,) = call(lead_kernel, "lead", [], [((8, 128), F32)], work=LEAD_WORK)
    (temp_copy,) = call(copy_kernel, "ahead", [temp_slab, lead], [slab])
    before = chip_step(temp_slab, 3)
    after = chip_step(temp_copy, 1)
    temp_sibling = sibling(temp_slab)
    stream_sibling = sibling(stream_slab)
    (part,) = call(
        part_kernel, "part", [stream_slab, probe], [((height, columns), F32)], work=2 * height * columns * local_rows
    )
    (before_copy,) = call(copy_kernel, "before", [before, part], [slab])
    before_sibling = sibling(before_copy)
    (message,) = call(
        gram_kernel,
        "gram",
        [part, temp_slab, temp_sibling, before, before_sibling, after],
        [((height, wide), F32)],
        work=4 * height * half * local_rows,
    )
    (beside,) = call(
        beside_kernel,
        "beside",
        [stream_slab, stream_sibling, before, after, message],
        [((3 * height, local_rows), BF16)],
    )
    beside = permute(beside, lambda n: (n - CORES if n % CORES == 0 else n + CORES) % groups)
    (message,) = call(add_kernel, "add", around(message, 1), [((height, wide), F32)])
    (message,) = call(
        functools.partial(sum_kernel, columns), "total", around(message, 4), [((height, packed), BF16)]
    )
    (across,) = call(relay_kernel, "relay", [beside, message], [slab])
    across = permute(across, lambda n: (n - CORES if n % CORES == 0 else n + CORES) % groups)
    (both,) = call(both_kernel, "both", [beside, after, message], [((4 * height, local_rows), BF16)])
    both_sibling = sibling(both)
    (message,) = call(collect_kernel, "collect", around(message, CORES, "samp"), [((half, packed), BF16)])
    message_other = sibling(message)
    (later,) = call(copy_kernel, "later", [across, message], [slab])
    across_sibling = sibling(later)
    (slabs,) = call(
        order_kernel,
        "order",
        [
            temp_slab, temp_sibling, before, before_sibling, after, stream_slab, stream_sibling,
            beside, both_sibling, across, across_sibling,
        ],
        [((2 * samples, local_rows), BF16)],
    )

    scales = (
        1.0 / (samples - 1.0),
        1.0 / ((samples - 1.0) * float(total_rows) ** 0.5),
        float(total_rows),
    )
    mine = columns // groups
    chunks = 4
    outs = (shape((columns, local_rows), BF16), shape((mine, local_rows), F32))
    basis, back_image = pl.pallas_call(
        functools.partial(output_kernel, columns, scales),
        out_shape=outs,
        in_specs=whole(3),
        out_specs=tuple([pl.BlockSpec(memory_space=pl.ANY)] * 2),
        scratch_shapes=[
            pltpu.VMEM((columns, samples), BF16),
            pltpu.VMEM((columns, samples), F32),
            pltpu.VMEM((columns, samples), F32),
            pltpu.VMEM((samples, packed), BF16),
            *[pltpu.VMEM(out.shape, out.dtype) for out in outs],
            pltpu.SemaphoreType.DMA((chunks + 1,)),
        ],
        compiler_params=params(40),
        cost_estimate=cost(2 * (columns + mine) * samples * local_rows, 7 << 20),
        name="outputs",
    )(message, message_other, slabs)
    return (basis, back_image)


def solution(mesh):
    return jax.shard_map(
        shards,
        mesh=mesh,
        in_specs=(P("samp", "rows"), P("samp", "rows"), P(None, "rows")),
        out_specs=(P(None, "rows"), P("samp", "rows")),
        check_vma=False,
    )
```

```python
import functools

import jax
import jax.numpy as jnp
from jax import lax
from jax.experimental import pallas as pl
from jax.experimental.pallas import tpu as pltpu
from jax.sharding import PartitionSpec as P

F32 = jnp.float32
BF16 = jnp.bfloat16
CORES = 2
SIDE = 4
LEAD_WORK = 1 << 33


def dot(left, right, dims):
    return lax.dot_general(left, right, (dims, ((), ())), preferred_element_type=F32)


def split3(value):
    high = value.astype(BF16)
    rest = value - high.astype(F32)
    mid = rest.astype(BF16)
    return high, mid, (rest - mid.astype(F32)).astype(BF16)


def params(mebibytes):
    return pltpu.CompilerParams(vmem_limit_bytes=mebibytes << 20)


def whole(count):
    return [pl.BlockSpec(memory_space=pltpu.VMEM)] * count


def cost(flops, traffic):
    return pl.CostEstimate(flops=flops, bytes_accessed=traffic, transcendentals=0)


def parity(row):
    return (row // SIDE + row % SIDE) % 2


def place(row, chip, role):
    return (row * SIDE + chip) * CORES + (role ^ parity(row))


def move(value, source):
    everyone = [
        (row, chip, role)
        for row in range(lax.axis_size("rows"))
        for chip in range(SIDE)
        for role in range(CORES)
    ]
    pairs = [(place(*source(*one)), place(*one)) for one in everyone]
    return lax.ppermute(value, ("rows", "samp"), pairs)


def chip_step(value, step):
    return move(value, lambda row, chip, role: (row, (chip + step) % SIDE, role ^ parity(row)))


def sibling(value):
    return move(value, lambda row, chip, role: (row, chip, 1 - role))


def beside_step(value):
    return move(value, lambda row, chip, role: (row, (chip + 2 * role - 1) % SIDE, role))


def around(value, axis):
    def source(step):
        def of(row, chip, role):
            z, y = divmod(row, SIDE)
            if axis == "y":
                return z * SIDE + (y + step) % SIDE, chip, role
            if axis == "z":
                return (z + step) % SIDE * SIDE + y, chip, role
            return row, (chip + step) % SIDE, 1 - role

        return of

    first, last, opposite = [move(value, source(step)) for step in (1, 3, 2)]
    return [value, first, last, opposite]


def whereabouts():
    own, row = lax.axis_index("samp"), lax.axis_index("rows")
    chip, core = own // CORES, lax.rem(own, CORES)
    return chip, core, lax.rem(core + row // SIDE + lax.rem(row, SIDE), 2)


def rows_at(place, height):
    return pl.ds(pl.multiple_of(place * height, height), height)


def by_role(own_ref, sibling_ref):
    _, core, role = whereabouts()
    own, other = own_ref[...], sibling_ref[...]
    return jnp.where(core == role, own, other), jnp.where(core == role, other, own)


def gram_kernel(
    part_ref, own_ref, sibling_ref, before_ref, before_sibling_ref, after_ref, message_ref
):
    height, columns = part_ref.shape
    chip, _, _ = whereabouts()
    mine = by_role(own_ref, sibling_ref)
    others = jnp.concatenate([mine[0], after_ref[...]], axis=0)
    near = dot(jnp.concatenate(mine, axis=0), others, ((1,), (1,)))
    place = lax.broadcasted_iota(jnp.int32, near.shape, 1) // height
    near = jnp.where(place == 0, 0.5 * near, near)
    half = rows_at(chip // 2, own_ref.shape[1] // 2)
    across = jnp.concatenate([before_ref[:, half], before_sibling_ref[:, half]], axis=0)
    across = dot(across, after_ref[:, half], ((1,), (1,)))
    gram = jnp.concatenate([near, across, jnp.zeros(across.shape, F32)], axis=1)
    gram = pltpu.roll(jnp.concatenate([gram, gram], axis=1), chip * height, 1)[:, : SIDE * height]
    message_ref[:, :columns] = part_ref[...]
    message_ref[:, columns:] = jnp.concatenate([gram[:height], gram[height:]], axis=1)


def collect_kernel(*refs):
    *blocks, out_ref = refs
    height = blocks[0].shape[0]
    chip, _, _ = whereabouts()
    for step, block in zip((0, 1, 3, 2), blocks):
        out_ref[rows_at(lax.rem(chip + step, SIDE), height), :] = block[...]


def lead_kernel(out_ref):
    out_ref[...] = jnp.zeros(out_ref.shape, F32)


def copy_kernel(value_ref, _, out_ref):
    out_ref[...] = value_ref[...]


def part_kernel(stream_ref, sibling_ref, probe_ref, part_ref):
    stream, _ = by_role(stream_ref, sibling_ref)
    part_ref[...] = dot(stream, probe_ref[...], ((1,), (1,)))


def beside_kernel(own_ref, sibling_ref, before_ref, after_ref, _, out_ref):
    height = own_ref.shape[0]
    _, core, role = whereabouts()
    out_ref[rows_at(core, height), :] = own_ref[...]
    out_ref[rows_at(1 - core, height), :] = sibling_ref[...]

    @pl.when(role == 0)
    def _():
        out_ref[CORES * height :] = before_ref[...]

    @pl.when(role == 1)
    def _():
        out_ref[CORES * height :] = after_ref[...]


def relay_kernel(beside_ref, _, out_ref):
    _, _, role = whereabouts()
    out_ref[...] = beside_ref[rows_at(role, out_ref.shape[0]), :]


def both_kernel(beside_ref, after_ref, across_ref, _, out_ref):
    height = after_ref.shape[0]
    out_ref[: -2 * height] = beside_ref[...]
    out_ref[-2 * height : -height] = after_ref[...]
    out_ref[-height:] = across_ref[...]


def order_kernel(
    temp_ref, temp_sibling_ref, before_ref, before_sibling_ref, after_ref, stream_ref, stream_sibling_ref,
    beside_ref, both_ref, across_ref, out_ref,
):
    chip, core, role = whereabouts()
    height = temp_ref.shape[0]

    def put(base, owner, step, value):
        place = (base * CORES + owner) * SIDE + lax.rem(chip + step, SIDE)
        out_ref[rows_at(place, height), :] = value

    rows = [slice(n * height, (n + 1) * height) for n in range(5)]
    put(0, core, 0, temp_ref[...])
    put(0, 1 - core, 0, temp_sibling_ref[...])
    put(0, role, SIDE - 1, before_ref[...])
    put(0, 1 - role, SIDE - 1, before_sibling_ref[...])
    put(0, role, 1, after_ref[...])
    put(0, 1 - role, 1, both_ref[rows[3]])
    put(0, role, 2, beside_ref[rows[2]])
    put(0, 1 - role, 2, both_ref[rows[2]])
    put(1, core, 0, stream_ref[...])
    put(1, 1 - core, 0, stream_sibling_ref[...])
    for n in range(CORES):
        put(1, n, SIDE - 1 - role * (SIDE - 2), beside_ref[rows[n]])
        put(1, n, 1 + role * (SIDE - 2), both_ref[rows[n]])
    put(1, role, 2, across_ref[...])
    put(1, 1 - role, 2, both_ref[rows[4]])


def add_kernel(a_ref, b_ref, c_ref, d_ref, out_ref):
    out_ref[...] = (a_ref[...] + b_ref[...]) + (c_ref[...] + d_ref[...])


def sum_kernel(columns, a_ref, b_ref, c_ref, d_ref, message_ref):
    total = (a_ref[...] + b_ref[...]) + (c_ref[...] + d_ref[...])
    pieces = [total[:, :columns].astype(BF16), *split3(total[:, columns:])]
    pieces = jnp.concatenate(pieces, axis=1)
    message_ref[...] = pieces


def output_kernel(columns, scales, *refs):
    near_ref, far_ref, slabs_ref, basis_ref, back_ref, left, gain, weights, message, basis, back, done = refs
    half = near_ref.shape[0]
    samples = CORES * half
    image_scale, back_scale, total_rows = scales
    own = lax.axis_index("samp")
    height = half // SIDE
    chip, _, role = whereabouts()
    for n in range(SIDE):
        owner = jnp.where(chip == n, role, 1 - role)
        rows = slice(n * height, (n + 1) * height)
        message[rows_at(owner * SIDE + n, height), :] = near_ref[rows]
        message[rows_at((1 - owner) * SIDE + n, height), :] = far_ref[rows]
    turned = message[:, :columns].astype(F32).T
    left[...] = turned.astype(BF16)
    products = sum(
        message[:, columns + n * samples : columns + (n + 1) * samples].astype(F32) for n in range(3)
    )
    first = lax.broadcasted_iota(jnp.int32, (half, samples), 1) < half
    top = jnp.where(first, products[:half], products[half:])
    bottom = jnp.where(first, products[half:], products[:half])
    bottom = jnp.concatenate([bottom[:, half:], bottom[:, :half]], axis=1)
    gram = jnp.concatenate([top, bottom], axis=0)
    row, lane = [lax.broadcasted_iota(jnp.int32, gram.shape, axis) // height for axis in (0, 1)]
    chips = half // height
    moves = lax.rem(lane + 2 * chips - row - 2, chips) == 0
    moved = jnp.where(moves, gram, 0.0)
    moved = jnp.concatenate(
        [moved[start : start + size] for base in (0, half) for start, size in ((base + height, half - height), (base, height))],
        axis=0,
    )
    ahead = jnp.concatenate([moved[:, height:], moved[:, :height]], axis=1)
    back_end = jnp.concatenate([moved[:, samples - half + height :], moved[:, : samples - half + height]], axis=1)
    moved = jnp.where(lax.rem(lane, chips) < chips - 1, ahead, back_end)
    gram = jnp.where(moves, 0.0, gram) + moved
    product = sum(dot(left[...], piece, ((1,), (0,))) for piece in split3(gram + gram.T))
    power = jnp.maximum(jnp.sum(product * turned, axis=1, keepdims=True), 0.0)
    power = power * (image_scale * image_scale)
    gain[...] = jnp.broadcast_to(
        image_scale * lax.rsqrt(power / total_rows + 1e-06), gain.shape
    )
    weights[...] = product * gain[...]

    chunks = done.shape[0] - 1
    height = columns // chunks
    copies = []
    for n in range(chunks):
        here = pl.ds(n * height, height)
        image = dot(left[here, :], slabs_ref[:samples, :], ((1,), (0,)))
        scale = jnp.concatenate([gain[here, :]] * (image.shape[1] // samples), axis=1)
        basis[here, :] = (image * scale).astype(BF16)
        copies.append(pltpu.make_async_copy(basis.at[here], basis_ref.at[here], done.at[n]))
        copies[-1].start()
    chosen = weights[rows_at(own, back.shape[0]), :].astype(BF16)
    back[...] = dot(chosen, slabs_ref[samples:, :], ((1,), (0,))) * back_scale
    copies.append(pltpu.make_async_copy(back, back_ref, done.at[chunks]))
    copies[-1].start()
    for copy in copies:
        copy.wait()


def shards(temp_slab, stream_slab, probe):
    height, local_rows = temp_slab.shape
    columns = probe.shape[0]
    groups = lax.axis_size("samp")
    row_groups = lax.axis_size("rows")
    total_rows = local_rows * row_groups
    samples = height * groups
    half = samples // CORES
    wide = columns + samples
    shape = jax.ShapeDtypeStruct

    def call(kernel, name, operands, outs, scratch=(), work=0):
        outs = [shape(*out) for out in outs]
        traffic = sum(value.size * value.dtype.itemsize for value in [*operands, *outs])
        return pl.pallas_call(
            kernel,
            out_shape=tuple(outs),
            in_specs=whole(len(operands)),
            out_specs=tuple(whole(len(outs))),
            scratch_shapes=[pltpu.VMEM(*one) for one in scratch],
            compiler_params=params(16),
            cost_estimate=cost(work, traffic),
            name=name,
        )(*operands)

    slab = ((height, local_rows), BF16)
    packed = columns + 3 * samples

    (lead,) = call(lead_kernel, "lead", [], [((8, 128), F32)], work=LEAD_WORK)
    (temp_copy,) = call(copy_kernel, "ahead", [temp_slab, lead], [slab])
    before = chip_step(temp_slab, 3)
    after = chip_step(temp_copy, 1)
    temp_sibling = sibling(temp_slab)
    stream_sibling = sibling(stream_slab)
    (part,) = call(
        part_kernel, "part", [stream_slab, stream_sibling, probe], [((height, columns), F32)], work=2 * height * columns * local_rows
    )
    (before_copy,) = call(copy_kernel, "before", [before, part], [slab])
    before_sibling = sibling(before_copy)
    (message,) = call(
        gram_kernel,
        "gram",
        [part, temp_slab, temp_sibling, before, before_sibling, after],
        [((height, wide), F32)],
        work=4 * height * half * local_rows,
    )
    (beside,) = call(
        beside_kernel,
        "beside",
        [stream_slab, stream_sibling, before, after, message],
        [((3 * height, local_rows), BF16)],
    )
    beside = beside_step(beside)
    (message,) = call(add_kernel, "add", around(message, "y"), [((height, wide), F32)])
    (across,) = call(relay_kernel, "relay", [beside, message], [slab])
    across = beside_step(across)
    (message,) = call(
        functools.partial(sum_kernel, columns), "total", around(message, "z"), [((height, packed), BF16)]
    )
    (both,) = call(both_kernel, "both", [beside, after, across, message], [((5 * height, local_rows), BF16)])
    both_sibling = sibling(both)
    (message,) = call(collect_kernel, "collect", around(message, "x"), [((half, packed), BF16)])
    message_other = sibling(message)
    (slabs,) = call(
        order_kernel,
        "order",
        [
            temp_slab, temp_sibling, before, before_sibling, after, stream_slab, stream_sibling,
            beside, both_sibling, across,
        ],
        [((2 * samples, local_rows), BF16)],
    )

    scales = (
        1.0 / (samples - 1.0),
        1.0 / ((samples - 1.0) * float(total_rows) ** 0.5),
        float(total_rows),
    )
    mine = columns // groups
    chunks = 4
    outs = (shape((columns, local_rows), BF16), shape((mine, local_rows), F32))
    basis, back_image = pl.pallas_call(
        functools.partial(output_kernel, columns, scales),
        out_shape=outs,
        in_specs=whole(3),
        out_specs=tuple([pl.BlockSpec(memory_space=pl.ANY)] * 2),
        scratch_shapes=[
            pltpu.VMEM((columns, samples), BF16),
            pltpu.VMEM((columns, samples), F32),
            pltpu.VMEM((columns, samples), F32),
            pltpu.VMEM((samples, packed), BF16),
            *[pltpu.VMEM(out.shape, out.dtype) for out in outs],
            pltpu.SemaphoreType.DMA((chunks + 1,)),
        ],
        compiler_params=params(40),
        cost_estimate=cost(2 * (columns + mine) * samples * local_rows, 7 << 20),
        name="outputs",
    )(message, message_other, slabs)
    return (basis, back_image)


def solution(mesh):
    return jax.shard_map(
        shards,
        mesh=mesh,
        in_specs=(P("samp", "rows"), P("samp", "rows"), P(None, "rows")),
        out_specs=(P(None, "rows"), P("samp", "rows")),
        check_vma=False,
    )
```

```python
import functools

import jax
import jax.numpy as jnp
from jax import lax
from jax.experimental import pallas as pl
from jax.experimental.pallas import tpu as pltpu
from jax.sharding import PartitionSpec as P

F32 = jnp.float32
BF16 = jnp.bfloat16
CORES = 2
SIDE = 4
LEAD_WORK = 1 << 33


def dot(left, right, dims):
    return lax.dot_general(left, right, (dims, ((), ())), preferred_element_type=F32)


def split3(value):
    high = value.astype(BF16)
    rest = value - high.astype(F32)
    mid = rest.astype(BF16)
    return high, mid, (rest - mid.astype(F32)).astype(BF16)


def params(mebibytes):
    return pltpu.CompilerParams(vmem_limit_bytes=mebibytes << 20)


def whole(count):
    return [pl.BlockSpec(memory_space=pltpu.VMEM)] * count


def cost(flops, traffic):
    return pl.CostEstimate(flops=flops, bytes_accessed=traffic, transcendentals=0)


def parity(row):
    return (row // SIDE + row % SIDE) % 2


def place(row, chip, role):
    return (row * SIDE + chip) * CORES + (role ^ parity(row))


def move(value, source):
    everyone = [
        (row, chip, role)
        for row in range(lax.axis_size("rows"))
        for chip in range(SIDE)
        for role in range(CORES)
    ]
    pairs = [(place(*source(*one)), place(*one)) for one in everyone]
    return lax.ppermute(value, ("rows", "samp"), pairs)


def chip_step(value, step):
    return move(value, lambda row, chip, role: (row, chip ^ step, role ^ parity(row)))


def sibling(value):
    return move(value, lambda row, chip, role: (row, chip, 1 - role))


def beside_step(value, flip):
    return move(value, lambda row, chip, role: (row, chip ^ (3 if role else 1), role ^ flip))


def around(value, axis):
    def source(step):
        def of(row, chip, role):
            z, y = divmod(row, SIDE)
            if axis == "y":
                return z * SIDE + (y ^ step), chip, role
            if axis == "z":
                return (z ^ step) * SIDE + y, chip, role
            return row, chip ^ step, 1 - role

        return of

    return [value] + [move(value, source(step)) for step in (1, 3, 2)]


def whereabouts():
    own, row = lax.axis_index("samp"), lax.axis_index("rows")
    chip, core = own // CORES, lax.rem(own, CORES)
    return chip, core, lax.rem(core + row // SIDE + lax.rem(row, SIDE), 2)


def rows_at(place, height):
    return pl.ds(pl.multiple_of(place * height, height), height)


def by_role(own_ref, sibling_ref):
    _, core, role = whereabouts()
    own, other = own_ref[...], sibling_ref[...]
    return jnp.where(core == role, own, other), jnp.where(core == role, other, own)


def gram_kernel(
    part_ref, own_ref, sibling_ref, other_ref, near_ref, near_sibling_ref, message_ref
):
    height, columns = part_ref.shape
    chip, _, _ = whereabouts()
    mine, other = by_role(own_ref, sibling_ref)
    both = jnp.concatenate([mine, other], axis=0)
    centre = 0.5 * dot(both, mine, ((1,), (1,)))
    span = own_ref.shape[1] // 2

    def half(number, *refs):
        rows = rows_at(number, span)
        blocks = [ref[:, rows] for ref in refs]
        return blocks[0] if len(blocks) == 1 else jnp.concatenate(blocks, axis=0)

    odd = lax.rem(chip, 2)
    core_first = whereabouts()[1] == whereabouts()[2]
    rows = half(odd, own_ref, sibling_ref)
    rows = jnp.where(core_first, rows, jnp.concatenate([rows[height:], rows[:height]], axis=0))
    sides = dot(rows, half(odd, near_ref, other_ref), ((1,), (1,)))
    across = dot(half(chip // 2, near_ref, near_sibling_ref), half(chip // 2, other_ref), ((1,), (1,)))
    pieces = []
    for n in range(SIDE):
        side = jnp.where(n == chip ^ 1, sides[:, :height], sides[:, height:])
        pieces.append(jnp.where(n == chip, centre, jnp.where(n == chip ^ 2, across, side)))
    gram = jnp.concatenate(pieces, axis=1)
    message_ref[:, :columns] = part_ref[...]
    message_ref[:, columns:] = jnp.concatenate([gram[:height], gram[height:]], axis=1)


def collect_kernel(*refs):
    *blocks, out_ref = refs
    height = blocks[0].shape[0]
    chip, _, _ = whereabouts()
    for step, block in zip((0, 1, 3, 2), blocks):
        out_ref[rows_at(chip ^ step, height), :] = block[...]


def lead_kernel(out_ref):
    out_ref[...] = jnp.zeros(out_ref.shape, F32)


def copy_kernel(value_ref, _, out_ref):
    out_ref[...] = value_ref[...]


def part_kernel(stream_ref, sibling_ref, probe_ref, part_ref):
    stream, _ = by_role(stream_ref, sibling_ref)
    part_ref[...] = dot(stream, probe_ref[...], ((1,), (1,)))


def beside_kernel(own_ref, sibling_ref, _, out_ref):
    height = own_ref.shape[0]
    _, core, _ = whereabouts()
    out_ref[rows_at(core, height), :] = own_ref[...]
    out_ref[rows_at(1 - core, height), :] = sibling_ref[...]


def relay_kernel(beside_ref, near_ref, other_ref, _, out_ref):
    height = near_ref.shape[0]
    _, _, role = whereabouts()
    out_ref[:height] = beside_ref[rows_at(1 - role, height), :]

    @pl.when(role == 0)
    def _():
        out_ref[height:] = near_ref[...]

    @pl.when(role == 1)
    def _():
        out_ref[height:] = other_ref[...]


def both_kernel(beside_ref, other_ref, across_ref, _, out_ref):
    height = other_ref.shape[0]
    out_ref[: 2 * height] = beside_ref[...]
    out_ref[2 * height : 3 * height] = other_ref[...]
    out_ref[3 * height :] = across_ref[...]


def order_kernel(
    temp_ref, temp_sibling_ref, near_ref, near_sibling_ref, other_ref, stream_ref, stream_sibling_ref,
    beside_ref, both_ref, across_ref, out_ref,
):
    chip, core, role = whereabouts()
    height = temp_ref.shape[0]

    def put(base, owner, place, value):
        place = (base * CORES + owner) * SIDE + place
        out_ref[rows_at(place, height), :] = value

    rows = [slice(n * height, (n + 1) * height) for n in range(5)]
    put(0, core, chip, temp_ref[...])
    put(0, 1 - core, chip, temp_sibling_ref[...])
    put(0, role, chip ^ 1, near_ref[...])
    put(0, 1 - role, chip ^ 1, near_sibling_ref[...])
    put(0, role, chip ^ 3, other_ref[...])
    put(0, 1 - role, chip ^ 3, both_ref[rows[2]])
    put(0, 1 - role, chip ^ 2, across_ref[rows[1]])
    put(0, role, chip ^ 2, both_ref[rows[4]])
    put(1, core, chip, stream_ref[...])
    put(1, 1 - core, chip, stream_sibling_ref[...])
    for n in range(CORES):
        put(1, n, chip ^ (1 + 2 * role), beside_ref[rows[n]])
        put(1, n, chip ^ (3 - 2 * role), both_ref[rows[n]])
    put(1, role, chip ^ 2, across_ref[rows[0]])
    put(1, 1 - role, chip ^ 2, both_ref[rows[3]])


def add_kernel(a_ref, b_ref, c_ref, d_ref, out_ref):
    out_ref[...] = (a_ref[...] + b_ref[...]) + (c_ref[...] + d_ref[...])


def sum_kernel(columns, a_ref, b_ref, c_ref, d_ref, message_ref):
    total = (a_ref[...] + b_ref[...]) + (c_ref[...] + d_ref[...])
    pieces = [total[:, :columns].astype(BF16), *split3(total[:, columns:])]
    pieces = jnp.concatenate(pieces, axis=1)
    message_ref[...] = pieces


def output_kernel(columns, scales, *refs):
    near_ref, far_ref, slabs_ref, basis_ref, back_ref, weights, message, basis, back, done = refs
    half = near_ref.shape[0]
    samples = CORES * half
    image_scale, back_scale, total_rows = scales
    own = lax.axis_index("samp")
    height = half // SIDE
    chip, _, role = whereabouts()
    for n in range(SIDE):
        owner = jnp.where(chip == n, role, 1 - role)
        rows = slice(n * height, (n + 1) * height)
        message[rows_at(owner * SIDE + n, height), :] = near_ref[rows]
        message[rows_at((1 - owner) * SIDE + n, height), :] = far_ref[rows]
    products = sum(
        message[:, columns + n * samples : columns + (n + 1) * samples].astype(F32) for n in range(3)
    )
    first = lax.broadcasted_iota(jnp.int32, (half, samples), 1) < half
    top = jnp.where(first, products[:half], products[half:])
    bottom = jnp.where(first, products[half:], products[:half])
    bottom = jnp.concatenate([bottom[:, half:], bottom[:, :half]], axis=1)
    gram = jnp.concatenate([top, bottom], axis=0)
    row, lane = [lax.broadcasted_iota(jnp.int32, gram.shape, axis) // height for axis in (0, 1)]
    moves = lax.rem(lane, SIDE) == lax.rem(row, SIDE) ^ 2
    moved = jnp.where(moves, gram, 0.0)
    moved = jnp.concatenate([moved[(n ^ 1) * height : ((n ^ 1) + 1) * height] for n in range(samples // height)], axis=0)
    ahead = jnp.concatenate([moved[:, height:], moved[:, :height]], axis=1)
    behind = jnp.concatenate([moved[:, -height:], moved[:, :-height]], axis=1)
    moved = jnp.where(lax.rem(lane, 2) == 0, ahead, behind)
    gram = jnp.where(moves, 0.0, gram) + moved
    pieces = split3(gram + gram.T)
    chunks = done.shape[0] - 1
    size = columns // chunks
    copies = []
    for n in range(chunks):
        here = pl.ds(n * size, size)
        turned = message[:, n * size : (n + 1) * size].astype(F32).T
        left = turned.astype(BF16)
        product = sum(dot(left, piece, ((1,), (0,))) for piece in pieces)
        power = jnp.maximum(jnp.sum(product * turned, axis=1, keepdims=True), 0.0)
        power = power * (image_scale * image_scale)
        gain = jnp.broadcast_to(image_scale * lax.rsqrt(power / total_rows + 1e-06), product.shape)
        weights[here, :] = product * gain
        image = dot(left, slabs_ref[:samples, :], ((1,), (0,)))
        basis[here, :] = (image * jnp.concatenate([gain] * (image.shape[1] // samples), axis=1)).astype(BF16)
        copies.append(pltpu.make_async_copy(basis.at[here], basis_ref.at[here], done.at[n]))
        copies[-1].start()
    chosen = weights[rows_at(own, back.shape[0]), :].astype(BF16)
    back[...] = dot(chosen, slabs_ref[samples:, :], ((1,), (0,))) * back_scale
    copies.append(pltpu.make_async_copy(back, back_ref, done.at[chunks]))
    copies[-1].start()
    for copy in copies:
        copy.wait()


def shards(temp_slab, stream_slab, probe):
    height, local_rows = temp_slab.shape
    columns = probe.shape[0]
    groups = lax.axis_size("samp")
    row_groups = lax.axis_size("rows")
    total_rows = local_rows * row_groups
    samples = height * groups
    half = samples // CORES
    wide = columns + samples
    shape = jax.ShapeDtypeStruct

    def call(kernel, name, operands, outs, scratch=(), work=0):
        outs = [shape(*out) for out in outs]
        traffic = sum(value.size * value.dtype.itemsize for value in [*operands, *outs])
        return pl.pallas_call(
            kernel,
            out_shape=tuple(outs),
            in_specs=whole(len(operands)),
            out_specs=tuple(whole(len(outs))),
            scratch_shapes=[pltpu.VMEM(*one) for one in scratch],
            compiler_params=params(16),
            cost_estimate=cost(work, traffic),
            name=name,
        )(*operands)

    slab = ((height, local_rows), BF16)
    packed = columns + 3 * samples

    (lead,) = call(lead_kernel, "lead", [], [((8, 128), F32)], work=LEAD_WORK)
    (temp_copy,) = call(copy_kernel, "ahead", [temp_slab, lead], [slab])
    near = chip_step(temp_slab, 1)
    other = chip_step(temp_slab, 3)
    temp_sibling = sibling(temp_copy)
    stream_sibling = sibling(stream_slab)
    (part,) = call(
        part_kernel, "part", [stream_slab, stream_sibling, probe], [((height, columns), F32)], work=2 * height * columns * local_rows
    )
    (near,) = call(copy_kernel, "near", [near, part], [slab], work=LEAD_WORK)
    (other,) = call(copy_kernel, "other", [other, part], [slab], work=LEAD_WORK)
    near_sibling = sibling(near)
    (message,) = call(
        gram_kernel,
        "gram",
        [part, temp_slab, temp_sibling, other, near, near_sibling],
        [((height, wide), F32)],
        work=4 * height * half * local_rows,
    )
    (beside,) = call(
        beside_kernel,
        "beside",
        [stream_slab, stream_sibling, temp_sibling],
        [((2 * height, local_rows), BF16)],
    )
    beside = beside_step(beside, 0)
    (message,) = call(add_kernel, "add", around(message, "y"), [((height, wide), F32)])
    (across,) = call(relay_kernel, "relay", [beside, near, other, message], [((2 * height, local_rows), BF16)])
    across = beside_step(across, 1)
    (message,) = call(
        functools.partial(sum_kernel, columns), "total", around(message, "z"), [((height, packed), BF16)]
    )
    (both,) = call(both_kernel, "both", [beside, other, across, message], [((5 * height, local_rows), BF16)])
    both_sibling = sibling(both)
    (message,) = call(collect_kernel, "collect", around(message, "x"), [((half, packed), BF16)])
    message_other = sibling(message)
    (slabs,) = call(
        order_kernel,
        "order",
        [
            temp_slab, temp_sibling, near, near_sibling, other, stream_slab, stream_sibling,
            beside, both_sibling, across,
        ],
        [((2 * samples, local_rows), BF16)],
    )

    scales = (
        1.0 / (samples - 1.0),
        1.0 / ((samples - 1.0) * float(total_rows) ** 0.5),
        float(total_rows),
    )
    mine = columns // groups
    chunks = 4
    outs = (shape((columns, local_rows), BF16), shape((mine, local_rows), F32))
    basis, back_image = pl.pallas_call(
        functools.partial(output_kernel, columns, scales),
        out_shape=outs,
        in_specs=whole(3),
        out_specs=tuple([pl.BlockSpec(memory_space=pl.ANY)] * 2),
        scratch_shapes=[
            pltpu.VMEM((columns, samples), F32),
            pltpu.VMEM((samples, packed), BF16),
            *[pltpu.VMEM(out.shape, out.dtype) for out in outs],
            pltpu.SemaphoreType.DMA((chunks + 1,)),
        ],
        compiler_params=params(40),
        cost_estimate=cost(2 * (columns + mine) * samples * local_rows, 7 << 20),
        name="outputs",
    )(message, message_other, slabs)
    return (basis, back_image)


def solution(mesh):
    return jax.shard_map(
        shards,
        mesh=mesh,
        in_specs=(P("samp", "rows"), P("samp", "rows"), P(None, "rows")),
        out_specs=(P(None, "rows"), P("samp", "rows")),
        check_vma=False,
    )
```

```python
import functools

import jax
import jax.numpy as jnp
from jax import lax
from jax.experimental import pallas as pl
from jax.experimental.pallas import tpu as pltpu
from jax.sharding import PartitionSpec as P

F32 = jnp.float32
BF16 = jnp.bfloat16
CORES = 2
SIDE = 4
LEAD_WORK = 1 << 33


def dot(left, right, dims):
    return lax.dot_general(left, right, (dims, ((), ())), preferred_element_type=F32)


def split3(value):
    high = value.astype(BF16)
    rest = value - high.astype(F32)
    mid = rest.astype(BF16)
    return high, mid, (rest - mid.astype(F32)).astype(BF16)


def params(mebibytes):
    return pltpu.CompilerParams(vmem_limit_bytes=mebibytes << 20)


def whole(count):
    return [pl.BlockSpec(memory_space=pltpu.VMEM)] * count


def cost(flops, traffic):
    return pl.CostEstimate(flops=flops, bytes_accessed=traffic, transcendentals=0)


def parity(row):
    return (row // SIDE + row % SIDE) % 2


def place(row, chip, role):
    return (row * SIDE + chip) * CORES + (role ^ parity(row))


def move(value, source):
    everyone = [
        (row, chip, role)
        for row in range(lax.axis_size("rows"))
        for chip in range(SIDE)
        for role in range(CORES)
    ]
    pairs = [(place(*source(*one)), place(*one)) for one in everyone]
    return lax.ppermute(value, ("rows", "samp"), pairs)


def chip_step(value, step):
    return move(value, lambda row, chip, role: (row, chip ^ step, role ^ parity(row)))


def sibling(value):
    return move(value, lambda row, chip, role: (row, chip, 1 - role))


def beside_step(value, flip):
    return move(value, lambda row, chip, role: (row, chip ^ (3 if role else 1), role ^ flip))


def around(value, axis):
    def source(step):
        def of(row, chip, role):
            z, y = divmod(row, SIDE)
            if axis == "y":
                return z * SIDE + (y ^ step), chip, role
            if axis == "z":
                return (z ^ step) * SIDE + y, chip, role
            return row, chip ^ step, 1 - role

        return of

    return [value] + [move(value, source(step)) for step in (1, 3, 2)]


def whereabouts():
    own, row = lax.axis_index("samp"), lax.axis_index("rows")
    chip, core = own // CORES, lax.rem(own, CORES)
    return chip, core, lax.rem(core + row // SIDE + lax.rem(row, SIDE), 2)


def rows_at(place, height):
    return pl.ds(pl.multiple_of(place * height, height), height)


def by_role(own_ref, sibling_ref):
    _, core, role = whereabouts()
    own, other = own_ref[...], sibling_ref[...]
    return jnp.where(core == role, own, other), jnp.where(core == role, other, own)


def gram_kernel(
    part_ref, own_ref, sibling_ref, other_ref, near_ref, near_sibling_ref, message_ref
):
    height, columns = part_ref.shape
    chip, _, _ = whereabouts()
    mine, other = by_role(own_ref, sibling_ref)
    both = jnp.concatenate([mine, other], axis=0)
    centre = 0.5 * dot(both, mine, ((1,), (1,)))
    span = own_ref.shape[1] // 2

    def half(number, *refs):
        rows = rows_at(number, span)
        blocks = [ref[:, rows] for ref in refs]
        return blocks[0] if len(blocks) == 1 else jnp.concatenate(blocks, axis=0)

    odd = lax.rem(chip, 2)
    core_first = whereabouts()[1] == whereabouts()[2]
    rows = half(odd, own_ref, sibling_ref)
    rows = jnp.where(core_first, rows, jnp.concatenate([rows[height:], rows[:height]], axis=0))
    sides = dot(rows, half(odd, near_ref, other_ref), ((1,), (1,)))
    across = dot(half(chip // 2, near_ref, near_sibling_ref), half(chip // 2, other_ref), ((1,), (1,)))
    pieces = []
    for n in range(SIDE):
        side = jnp.where(n == chip ^ 1, sides[:, :height], sides[:, height:])
        pieces.append(jnp.where(n == chip, centre, jnp.where(n == chip ^ 2, across, side)))
    gram = jnp.concatenate(pieces, axis=1)
    message_ref[:, :columns] = part_ref[...]
    message_ref[:, columns:] = jnp.concatenate([gram[:height], gram[height:]], axis=1)


def collect_kernel(*refs):
    *blocks, out_ref = refs
    height = blocks[0].shape[0]
    chip, _, _ = whereabouts()
    for step, block in zip((0, 1, 3, 2), blocks):
        out_ref[rows_at(chip ^ step, height), :] = block[...]


def lead_kernel(out_ref):
    out_ref[...] = jnp.zeros(out_ref.shape, F32)


def copy_kernel(value_ref, _, out_ref):
    out_ref[...] = value_ref[...]


def part_kernel(stream_ref, sibling_ref, probe_ref, part_ref):
    stream, _ = by_role(stream_ref, sibling_ref)
    part_ref[...] = dot(stream, probe_ref[...], ((1,), (1,)))


def beside_kernel(own_ref, sibling_ref, _, out_ref):
    height = own_ref.shape[0]
    _, core, _ = whereabouts()
    out_ref[rows_at(core, height), :] = own_ref[...]
    out_ref[rows_at(1 - core, height), :] = sibling_ref[...]


def relay_kernel(beside_ref, near_ref, other_ref, _, out_ref):
    height = near_ref.shape[0]
    _, _, role = whereabouts()
    out_ref[:height] = beside_ref[rows_at(1 - role, height), :]

    @pl.when(role == 0)
    def _():
        out_ref[height:] = near_ref[...]

    @pl.when(role == 1)
    def _():
        out_ref[height:] = other_ref[...]


def both_kernel(beside_ref, other_ref, across_ref, _, out_ref):
    height = other_ref.shape[0]
    out_ref[: 2 * height] = beside_ref[...]
    out_ref[2 * height : 3 * height] = other_ref[...]
    out_ref[3 * height :] = across_ref[...]


def order_kernel(
    temp_ref, temp_sibling_ref, near_ref, near_sibling_ref, other_ref, stream_ref, stream_sibling_ref,
    beside_ref, both_ref, across_ref, out_ref,
):
    chip, core, role = whereabouts()
    height = temp_ref.shape[0]

    def put(base, owner, place, value):
        place = (base * CORES + owner) * SIDE + place
        out_ref[rows_at(place, height), :] = value

    rows = [slice(n * height, (n + 1) * height) for n in range(5)]
    put(0, core, chip, temp_ref[...])
    put(0, 1 - core, chip, temp_sibling_ref[...])
    put(0, role, chip ^ 1, near_ref[...])
    put(0, 1 - role, chip ^ 1, near_sibling_ref[...])
    put(0, role, chip ^ 3, other_ref[...])
    put(0, 1 - role, chip ^ 3, both_ref[rows[2]])
    put(0, 1 - role, chip ^ 2, across_ref[rows[1]])
    put(0, role, chip ^ 2, both_ref[rows[4]])
    put(1, core, chip, stream_ref[...])
    put(1, 1 - core, chip, stream_sibling_ref[...])
    for n in range(CORES):
        put(1, n, chip ^ (1 + 2 * role), beside_ref[rows[n]])
        put(1, n, chip ^ (3 - 2 * role), both_ref[rows[n]])
    put(1, role, chip ^ 2, across_ref[rows[0]])
    put(1, 1 - role, chip ^ 2, both_ref[rows[3]])


def add_kernel(a_ref, b_ref, c_ref, d_ref, out_ref):
    out_ref[...] = (a_ref[...] + b_ref[...]) + (c_ref[...] + d_ref[...])


def sum_kernel(columns, a_ref, b_ref, c_ref, d_ref, message_ref):
    total = (a_ref[...] + b_ref[...]) + (c_ref[...] + d_ref[...])
    pieces = [total[:, :columns].astype(BF16), *split3(total[:, columns:])]
    pieces = jnp.concatenate(pieces, axis=1)
    message_ref[...] = pieces


def output_kernel(columns, scales, *refs):
    near_ref, far_ref, slabs_ref, basis_ref, back_ref, weights, message, basis, back, done = refs
    half = near_ref.shape[0]
    samples = CORES * half
    image_scale, back_scale, total_rows = scales
    own = lax.axis_index("samp")
    height = half // SIDE
    chip, _, role = whereabouts()
    for n in range(SIDE):
        owner = jnp.where(chip == n, role, 1 - role)
        rows = slice(n * height, (n + 1) * height)
        message[rows_at(owner * SIDE + n, height), :] = near_ref[rows]
        message[rows_at((1 - owner) * SIDE + n, height), :] = far_ref[rows]
    products = sum(
        message[:, columns + n * samples : columns + (n + 1) * samples].astype(F32) for n in range(3)
    )
    first = lax.broadcasted_iota(jnp.int32, (half, samples), 1) < half
    top = jnp.where(first, products[:half], products[half:])
    bottom = jnp.where(first, products[half:], products[:half])
    bottom = jnp.concatenate([bottom[:, half:], bottom[:, :half]], axis=1)
    gram = jnp.concatenate([top, bottom], axis=0)
    row, lane = [lax.broadcasted_iota(jnp.int32, gram.shape, axis) // height for axis in (0, 1)]
    moves = lax.rem(lane, SIDE) == lax.rem(row, SIDE) ^ 2
    moved = jnp.where(moves, gram, 0.0)
    moved = jnp.concatenate([moved[(n ^ 1) * height : ((n ^ 1) + 1) * height] for n in range(samples // height)], axis=0)
    ahead = jnp.concatenate([moved[:, height:], moved[:, :height]], axis=1)
    behind = jnp.concatenate([moved[:, -height:], moved[:, :-height]], axis=1)
    moved = jnp.where(lax.rem(lane, 2) == 0, ahead, behind)
    gram = jnp.where(moves, 0.0, gram) + moved
    pieces = split3(gram + gram.T)
    chunks = done.shape[0] - 2
    size = columns // chunks
    copies = []
    for n in range(chunks):
        here = pl.ds(n * size, size)
        turned = message[:, n * size : (n + 1) * size].astype(F32).T
        left = turned.astype(BF16)
        product = sum(dot(left, piece, ((1,), (0,))) for piece in pieces)
        power = jnp.maximum(jnp.sum(product * turned, axis=1, keepdims=True), 0.0)
        power = power * (image_scale * image_scale)
        gain = jnp.broadcast_to(image_scale * lax.rsqrt(power / total_rows + 1e-06), product.shape)
        weights[here, :] = product * gain
        step = size if n else size // 2
        for start in range(0, size, step):
            rows = slice(start, start + step)
            here = pl.ds(n * size + start, step)
            image = dot(left[rows], slabs_ref[:samples, :], ((1,), (0,)))
            scale = jnp.concatenate([gain[rows]] * (image.shape[1] // samples), axis=1)
            basis[here, :] = (image * scale).astype(BF16)
            copies.append(pltpu.make_async_copy(basis.at[here], basis_ref.at[here], done.at[len(copies)]))
            copies[-1].start()
    chosen = weights[rows_at(own, back.shape[0]), :].astype(BF16)
    back[...] = dot(chosen, slabs_ref[samples:, :], ((1,), (0,))) * back_scale
    copies.append(pltpu.make_async_copy(back, back_ref, done.at[len(copies)]))
    copies[-1].start()
    for copy in copies:
        copy.wait()


def shards(temp_slab, stream_slab, probe):
    height, local_rows = temp_slab.shape
    columns = probe.shape[0]
    groups = lax.axis_size("samp")
    row_groups = lax.axis_size("rows")
    total_rows = local_rows * row_groups
    samples = height * groups
    half = samples // CORES
    wide = columns + samples
    shape = jax.ShapeDtypeStruct

    def call(kernel, name, operands, outs, scratch=(), work=0):
        outs = [shape(*out) for out in outs]
        traffic = sum(value.size * value.dtype.itemsize for value in [*operands, *outs])
        return pl.pallas_call(
            kernel,
            out_shape=tuple(outs),
            in_specs=whole(len(operands)),
            out_specs=tuple(whole(len(outs))),
            scratch_shapes=[pltpu.VMEM(*one) for one in scratch],
            compiler_params=params(16),
            cost_estimate=cost(work, traffic),
            name=name,
        )(*operands)

    slab = ((height, local_rows), BF16)
    packed = columns + 3 * samples

    (lead,) = call(lead_kernel, "lead", [], [((8, 128), F32)], work=LEAD_WORK)
    (temp_copy,) = call(copy_kernel, "ahead", [temp_slab, lead], [slab])
    near = chip_step(temp_slab, 1)
    other = chip_step(temp_slab, 3)
    temp_sibling = sibling(temp_copy)
    stream_sibling = sibling(stream_slab)
    (part,) = call(
        part_kernel, "part", [stream_slab, stream_sibling, probe], [((height, columns), F32)], work=2 * height * columns * local_rows
    )
    (near,) = call(copy_kernel, "near", [near, part], [slab], work=LEAD_WORK)
    (other,) = call(copy_kernel, "other", [other, part], [slab], work=LEAD_WORK)
    near_sibling = sibling(near)
    (message,) = call(
        gram_kernel,
        "gram",
        [part, temp_slab, temp_sibling, other, near, near_sibling],
        [((height, wide), F32)],
        work=4 * height * half * local_rows,
    )
    (beside,) = call(
        beside_kernel,
        "beside",
        [stream_slab, stream_sibling, temp_sibling],
        [((2 * height, local_rows), BF16)],
    )
    beside = beside_step(beside, 1)
    (message,) = call(add_kernel, "add", around(message, "y"), [((height, wide), F32)])
    (across,) = call(relay_kernel, "relay", [beside, near, other, message], [((2 * height, local_rows), BF16)])
    across = beside_step(across, 1)
    (message,) = call(
        functools.partial(sum_kernel, columns), "total", around(message, "z"), [((height, packed), BF16)]
    )
    (both,) = call(both_kernel, "both", [beside, other, across, message], [((5 * height, local_rows), BF16)])
    both_sibling = sibling(both)
    (message,) = call(collect_kernel, "collect", around(message, "x"), [((half, packed), BF16)])
    message_other = sibling(message)
    (slabs,) = call(
        order_kernel,
        "order",
        [
            temp_slab, temp_sibling, near, near_sibling, other, stream_slab, stream_sibling,
            beside, both_sibling, across,
        ],
        [((2 * samples, local_rows), BF16)],
    )

    scales = (
        1.0 / (samples - 1.0),
        1.0 / ((samples - 1.0) * float(total_rows) ** 0.5),
        float(total_rows),
    )
    mine = columns // groups
    chunks = 4
    outs = (shape((columns, local_rows), BF16), shape((mine, local_rows), F32))
    basis, back_image = pl.pallas_call(
        functools.partial(output_kernel, columns, scales),
        out_shape=outs,
        in_specs=whole(3),
        out_specs=tuple([pl.BlockSpec(memory_space=pl.ANY)] * 2),
        scratch_shapes=[
            pltpu.VMEM((columns, samples), F32),
            pltpu.VMEM((samples, packed), BF16),
            *[pltpu.VMEM(out.shape, out.dtype) for out in outs],
            pltpu.SemaphoreType.DMA((chunks + 2,)),
        ],
        compiler_params=params(40),
        cost_estimate=cost(2 * (columns + mine) * samples * local_rows, 7 << 20),
        name="outputs",
    )(message, message_other, slabs)
    return (basis, back_image)


def solution(mesh):
    return jax.shard_map(
        shards,
        mesh=mesh,
        in_specs=(P("samp", "rows"), P("samp", "rows"), P(None, "rows")),
        out_specs=(P(None, "rows"), P("samp", "rows")),
        check_vma=False,
    )
```

```python
import functools

import jax
import jax.numpy as jnp
from jax import lax
from jax.experimental import pallas as pl
from jax.experimental.pallas import tpu as pltpu
from jax.sharding import PartitionSpec as P

F32 = jnp.float32
BF16 = jnp.bfloat16
CORES = 2
SIDE = 4
LEAD_WORK = 1 << 33


def dot(left, right, dims):
    return lax.dot_general(left, right, (dims, ((), ())), preferred_element_type=F32)


def split3(value):
    high = value.astype(BF16)
    rest = value - high.astype(F32)
    mid = rest.astype(BF16)
    return high, mid, (rest - mid.astype(F32)).astype(BF16)


def params(mebibytes):
    return pltpu.CompilerParams(vmem_limit_bytes=mebibytes << 20)


def whole(count):
    return [pl.BlockSpec(memory_space=pltpu.VMEM)] * count


def cost(flops, traffic):
    return pl.CostEstimate(flops=flops, bytes_accessed=traffic, transcendentals=0)


def parity(row):
    return (row // SIDE + row % SIDE) % 2


def place(row, chip, role):
    return (row * SIDE + chip) * CORES + (role ^ parity(row))


def move(value, source):
    everyone = [
        (row, chip, role)
        for row in range(lax.axis_size("rows"))
        for chip in range(SIDE)
        for role in range(CORES)
    ]
    pairs = [(place(*source(*one)), place(*one)) for one in everyone]
    return lax.ppermute(value, ("rows", "samp"), pairs)


def chip_step(value, step):
    return move(value, lambda row, chip, role: (row, chip ^ step, role ^ parity(row)))


def sibling(value):
    return move(value, lambda row, chip, role: (row, chip, 1 - role))


def beside_step(value, flip):
    return move(value, lambda row, chip, role: (row, chip ^ (3 if role else 1), role ^ flip))


def around(value, axis):
    def source(step):
        def of(row, chip, role):
            z, y = divmod(row, SIDE)
            if axis == "y":
                return z * SIDE + (y ^ step), chip, role
            if axis == "z":
                return (z ^ step) * SIDE + y, chip, role
            return row, chip ^ step, 1 - role

        return of

    return [value] + [move(value, source(step)) for step in (1, 3, 2)]


def whereabouts():
    own, row = lax.axis_index("samp"), lax.axis_index("rows")
    chip, core = own // CORES, lax.rem(own, CORES)
    return chip, core, lax.rem(core + row // SIDE + lax.rem(row, SIDE), 2)


def rows_at(place, height):
    return pl.ds(pl.multiple_of(place * height, height), height)


def by_role(own_ref, sibling_ref):
    _, core, role = whereabouts()
    own, other = own_ref[...], sibling_ref[...]
    return jnp.where(core == role, own, other), jnp.where(core == role, other, own)


def gram_kernel(
    part_ref, own_ref, sibling_ref, other_ref, near_ref, near_sibling_ref, message_ref
):
    height, columns = part_ref.shape
    chip, _, _ = whereabouts()
    mine, other = by_role(own_ref, sibling_ref)
    both = jnp.concatenate([mine, other], axis=0)
    centre = 0.5 * dot(both, mine, ((1,), (1,)))
    span = own_ref.shape[1] // 2

    def half(number, *refs):
        rows = rows_at(number, span)
        blocks = [ref[:, rows] for ref in refs]
        return blocks[0] if len(blocks) == 1 else jnp.concatenate(blocks, axis=0)

    odd = lax.rem(chip, 2)
    core_first = whereabouts()[1] == whereabouts()[2]
    rows = half(odd, own_ref, sibling_ref)
    rows = jnp.where(core_first, rows, jnp.concatenate([rows[height:], rows[:height]], axis=0))
    sides = dot(rows, half(odd, near_ref, other_ref), ((1,), (1,)))
    across = dot(half(chip // 2, near_ref, near_sibling_ref), half(chip // 2, other_ref), ((1,), (1,)))
    pieces = []
    for n in range(SIDE):
        side = jnp.where(n == chip ^ 1, sides[:, :height], sides[:, height:])
        pieces.append(jnp.where(n == chip, centre, jnp.where(n == chip ^ 2, across, side)))
    gram = jnp.concatenate(pieces, axis=1)
    message_ref[:, :columns] = part_ref[...]
    message_ref[:, columns:] = jnp.concatenate([gram[:height], gram[height:]], axis=1)


def collect_kernel(*refs):
    *blocks, out_ref = refs
    height = blocks[0].shape[0]
    chip, _, _ = whereabouts()
    for step, block in zip((0, 1, 3, 2), blocks):
        out_ref[rows_at(chip ^ step, height), :] = block[...]


def lead_kernel(out_ref):
    out_ref[...] = jnp.zeros(out_ref.shape, F32)


def copy_kernel(value_ref, _, out_ref):
    out_ref[...] = value_ref[...]


def part_kernel(stream_ref, sibling_ref, probe_ref, part_ref):
    stream, _ = by_role(stream_ref, sibling_ref)
    part_ref[...] = dot(stream, probe_ref[...], ((1,), (1,)))


def beside_kernel(own_ref, sibling_ref, _, out_ref):
    height = own_ref.shape[0]
    _, core, _ = whereabouts()
    out_ref[rows_at(core, height), :] = own_ref[...]
    out_ref[rows_at(1 - core, height), :] = sibling_ref[...]


def relay_kernel(beside_ref, near_ref, other_ref, _, out_ref):
    height = near_ref.shape[0]
    _, _, role = whereabouts()
    out_ref[:height] = beside_ref[rows_at(1 - role, height), :]

    @pl.when(role == 0)
    def _():
        out_ref[height:] = near_ref[...]

    @pl.when(role == 1)
    def _():
        out_ref[height:] = other_ref[...]


def both_kernel(beside_ref, other_ref, across_ref, _, out_ref):
    height = other_ref.shape[0]
    out_ref[: 2 * height] = beside_ref[...]
    out_ref[2 * height : 3 * height] = other_ref[...]
    out_ref[3 * height :] = across_ref[...]


def order_kernel(
    temp_ref, temp_sibling_ref, near_ref, near_sibling_ref, other_ref, stream_ref, stream_sibling_ref,
    beside_ref, both_ref, across_ref, out_ref,
):
    chip, core, role = whereabouts()
    height = temp_ref.shape[0]

    def put(base, owner, place, value):
        place = (base * CORES + owner) * SIDE + place
        out_ref[rows_at(place, height), :] = value

    rows = [slice(n * height, (n + 1) * height) for n in range(5)]
    put(0, core, chip, temp_ref[...])
    put(0, 1 - core, chip, temp_sibling_ref[...])
    put(0, role, chip ^ 1, near_ref[...])
    put(0, 1 - role, chip ^ 1, near_sibling_ref[...])
    put(0, role, chip ^ 3, other_ref[...])
    put(0, 1 - role, chip ^ 3, both_ref[rows[2]])
    put(0, 1 - role, chip ^ 2, across_ref[rows[1]])
    put(0, role, chip ^ 2, both_ref[rows[4]])
    put(1, core, chip, stream_ref[...])
    put(1, 1 - core, chip, stream_sibling_ref[...])
    for n in range(CORES):
        put(1, n, chip ^ (1 + 2 * role), beside_ref[rows[n]])
        put(1, n, chip ^ (3 - 2 * role), both_ref[rows[n]])
    put(1, role, chip ^ 2, across_ref[rows[0]])
    put(1, 1 - role, chip ^ 2, both_ref[rows[3]])


def add_kernel(a_ref, b_ref, c_ref, d_ref, out_ref):
    out_ref[...] = (a_ref[...] + b_ref[...]) + (c_ref[...] + d_ref[...])


def sum_kernel(columns, a_ref, b_ref, c_ref, d_ref, message_ref):
    total = (a_ref[...] + b_ref[...]) + (c_ref[...] + d_ref[...])
    pieces = [total[:, :columns].astype(BF16), *split3(total[:, columns:])]
    pieces = jnp.concatenate(pieces, axis=1)
    message_ref[...] = pieces


def output_kernel(columns, scales, *refs):
    near_ref, far_ref, slabs_ref, basis_ref, back_ref, weights, message, basis, back, done = refs
    half = near_ref.shape[0]
    samples = CORES * half
    image_scale, back_scale, total_rows = scales
    own = lax.axis_index("samp")
    height = half // SIDE
    chip, _, role = whereabouts()
    for n in range(SIDE):
        owner = jnp.where(chip == n, role, 1 - role)
        rows = slice(n * height, (n + 1) * height)
        message[rows_at(owner * SIDE + n, height), :] = near_ref[rows]
        message[rows_at((1 - owner) * SIDE + n, height), :] = far_ref[rows]
    products = sum(
        message[:, columns + n * samples : columns + (n + 1) * samples].astype(F32) for n in range(3)
    )
    first = lax.broadcasted_iota(jnp.int32, (half, samples), 1) < half
    top = jnp.where(first, products[:half], products[half:])
    bottom = jnp.where(first, products[half:], products[:half])
    bottom = jnp.concatenate([bottom[:, half:], bottom[:, :half]], axis=1)
    gram = jnp.concatenate([top, bottom], axis=0)
    row, lane = [lax.broadcasted_iota(jnp.int32, gram.shape, axis) // height for axis in (0, 1)]
    moves = lax.rem(lane, SIDE) == lax.rem(row, SIDE) ^ 2
    moved = jnp.where(moves, gram, 0.0)
    moved = jnp.concatenate([moved[(n ^ 1) * height : ((n ^ 1) + 1) * height] for n in range(samples // height)], axis=0)
    ahead = jnp.concatenate([moved[:, height:], moved[:, :height]], axis=1)
    behind = jnp.concatenate([moved[:, -height:], moved[:, :-height]], axis=1)
    moved = jnp.where(lax.rem(lane, 2) == 0, ahead, behind)
    gram = jnp.where(moves, 0.0, gram) + moved
    pieces = split3(gram + gram.T)
    chunks = done.shape[0] - 2
    size = columns // chunks
    copies = []
    for n in range(chunks):
        here = pl.ds(n * size, size)
        turned = message[:, n * size : (n + 1) * size].astype(F32).T
        left = turned.astype(BF16)
        product = sum(dot(left, piece, ((1,), (0,))) for piece in pieces)
        power = jnp.maximum(jnp.sum(product * turned, axis=1, keepdims=True), 0.0)
        power = power * (image_scale * image_scale)
        gain = jnp.broadcast_to(image_scale * lax.rsqrt(power / total_rows + 1e-06), product.shape)
        weights[here, :] = product * gain
        step = size if n else size // 2
        for start in range(0, size, step):
            rows = slice(start, start + step)
            here = pl.ds(n * size + start, step)
            image = dot(left[rows], slabs_ref[:samples, :], ((1,), (0,)))
            scale = jnp.concatenate([gain[rows]] * (image.shape[1] // samples), axis=1)
            basis[here, :] = (image * scale).astype(BF16)
            copies.append(pltpu.make_async_copy(basis.at[here], basis_ref.at[here], done.at[len(copies)]))
            copies[-1].start()
    chosen = weights[rows_at(own, back.shape[0]), :].astype(BF16)
    back[...] = dot(chosen, slabs_ref[samples:, :], ((1,), (0,))) * back_scale
    copies.append(pltpu.make_async_copy(back, back_ref, done.at[len(copies)]))
    copies[-1].start()
    for copy in copies:
        copy.wait()


def shards(temp_slab, stream_slab, probe):
    height, local_rows = temp_slab.shape
    columns = probe.shape[0]
    groups = lax.axis_size("samp")
    row_groups = lax.axis_size("rows")
    total_rows = local_rows * row_groups
    samples = height * groups
    half = samples // CORES
    wide = columns + samples
    shape = jax.ShapeDtypeStruct

    def call(kernel, name, operands, outs, scratch=(), work=0):
        outs = [shape(*out) for out in outs]
        traffic = sum(value.size * value.dtype.itemsize for value in [*operands, *outs])
        return pl.pallas_call(
            kernel,
            out_shape=tuple(outs),
            in_specs=whole(len(operands)),
            out_specs=tuple(whole(len(outs))),
            scratch_shapes=[pltpu.VMEM(*one) for one in scratch],
            compiler_params=params(16),
            cost_estimate=cost(work, traffic),
            name=name,
        )(*operands)

    slab = ((height, local_rows), BF16)
    packed = columns + 3 * samples

    (lead,) = call(lead_kernel, "lead", [], [((8, 128), F32)], work=LEAD_WORK)
    (temp_copy,) = call(copy_kernel, "ahead", [temp_slab, lead], [slab])
    near = chip_step(temp_slab, 1)
    other = chip_step(temp_slab, 3)
    temp_sibling = sibling(temp_copy)
    stream_sibling = sibling(stream_slab)
    (part,) = call(
        part_kernel, "part", [stream_slab, stream_sibling, probe], [((height, columns), F32)], work=2 * height * columns * local_rows
    )
    (near,) = call(copy_kernel, "near", [near, part], [slab], work=LEAD_WORK)
    (other,) = call(copy_kernel, "other", [other, near], [slab], work=LEAD_WORK)
    near_sibling = sibling(near)
    (message,) = call(
        gram_kernel,
        "gram",
        [part, temp_slab, temp_sibling, other, near, near_sibling],
        [((height, wide), F32)],
        work=4 * height * half * local_rows,
    )
    (beside,) = call(
        beside_kernel,
        "beside",
        [stream_slab, stream_sibling, temp_sibling],
        [((2 * height, local_rows), BF16)],
    )
    beside = beside_step(beside, 1)
    (message,) = call(add_kernel, "add", around(message, "z"), [((height, wide), F32)])
    (across,) = call(relay_kernel, "relay", [beside, near, other, message], [((2 * height, local_rows), BF16)])
    across = beside_step(across, 1)
    (message,) = call(
        functools.partial(sum_kernel, columns), "total", around(message, "y"), [((height, packed), BF16)]
    )
    (both,) = call(both_kernel, "both", [beside, other, across, message], [((5 * height, local_rows), BF16)])
    both_sibling = sibling(both)
    (message,) = call(collect_kernel, "collect", around(message, "x"), [((half, packed), BF16)])
    message_other = sibling(message)
    (slabs,) = call(
        order_kernel,
        "order",
        [
            temp_slab, temp_sibling, near, near_sibling, other, stream_slab, stream_sibling,
            beside, both_sibling, across,
        ],
        [((2 * samples, local_rows), BF16)],
    )

    scales = (
        1.0 / (samples - 1.0),
        1.0 / ((samples - 1.0) * float(total_rows) ** 0.5),
        float(total_rows),
    )
    mine = columns // groups
    chunks = 4
    outs = (shape((columns, local_rows), BF16), shape((mine, local_rows), F32))
    basis, back_image = pl.pallas_call(
        functools.partial(output_kernel, columns, scales),
        out_shape=outs,
        in_specs=whole(3),
        out_specs=tuple([pl.BlockSpec(memory_space=pl.ANY)] * 2),
        scratch_shapes=[
            pltpu.VMEM((columns, samples), F32),
            pltpu.VMEM((samples, packed), BF16),
            *[pltpu.VMEM(out.shape, out.dtype) for out in outs],
            pltpu.SemaphoreType.DMA((chunks + 2,)),
        ],
        compiler_params=params(40),
        cost_estimate=cost(2 * (columns + mine) * samples * local_rows, 7 << 20),
        name="outputs",
    )(message, message_other, slabs)
    return (basis, back_image)


def solution(mesh):
    return jax.shard_map(
        shards,
        mesh=mesh,
        in_specs=(P("samp", "rows"), P("samp", "rows"), P(None, "rows")),
        out_specs=(P(None, "rows"), P("samp", "rows")),
        check_vma=False,
    )
```
